512 devices in a mesh: dp: 32 (over y, x), tensor: 16 (over z, core).
Axes of the slice: x: 4, y: 8, z: 8, core: 2. Of those that a mesh axis runs over, the one named last changes fastest.
Arguments:
- queries: bfloat16 [32, 256, 4096], P('dp', None, 'tensor'), may hold values from -16 to 16
- keys: bfloat16 [128, 192, 4096], P('dp', None, 'tensor'), may hold values from -16 to 16
- values: bfloat16 [128, 192, 4096], P('dp', None, 'tensor'), may hold values from -6 to 6
- cotangent: bfloat16 [32, 256, 4096], P('dp', None, 'tensor'), may hold values from -192 to 192
- passage_ids: int32 [32, 16], replicated, may hold values from 0 to 127, as said below
- store_slot: int32 [128], replicated, may hold values from 0 to 127, as said below
- lengths: int32 [128], replicated, may hold values from 128 to 192
Outputs:
- context: bfloat16 [32, 256, 4096], P('dp', None, 'tensor')
- grad_queries: bfloat16 [32, 256, 4096], P('dp', None, 'tensor')
- grad_keys: bfloat16 [128, 192, 4096], P('dp', None, 'tensor')
- grad_values: bfloat16 [128, 192, 4096], P('dp', None, 'tensor')
- relevance: float32 [128], P('dp')
The draws below stay inside these ranges and needn't reach their ends.
Inputs may be any that keep to these rules, and one draw needn't show every extreme that they name: `passage_ids`: each row names 16 different passages. No index of dp stores more than 1 passages of one row, and some row has 1 on one index. `store_slot`: A permutation of the storage positions.
All inputs are finite; a program needn't handle non-finite values.
Results may differ from the reference program's by a relative error of at most 0.0019.
The reference program's roundings to bfloat16 on the way (of `attention_low`, `grad_scores`, `key_grads`, `value_grads` and `passage_mass`) count: a program that leaves them out, or rounds other values in their place, can miss the bound.
Values may be sent and summed in bfloat16 or wider, within the bound.
A program may use at most 128 MiB of HBM per device.

```python
import jax
import jax.numpy as jnp
from jax import lax

D = 4096
HEADS = 64
TGT = 256
PLEN = 192
K_PASS = 16
P_DEV = 4
QUESTIONS = 32
PASSAGES = 128
PAIR_CAP = 1
N_DP = 32


def storage_order(key):
    return jax.random.permutation(jax.random.fold_in(key, 101), PASSAGES).astype(jnp.int32)


def draw_queries(key, part):
    key = jax.random.fold_in(key, 1)
    sampled_draw = jnp.clip(jax.random.normal(key, (QUESTIONS, TGT, D), jnp.float32), -6.0, 6.0)
    return sampled_draw.astype(jnp.bfloat16)


def draw_keys(key, part):
    key = jax.random.fold_in(key, 2)
    sampled_draw = jnp.clip(jax.random.normal(key, (PASSAGES, PLEN, D), jnp.float32), -6.0, 6.0)
    return sampled_draw.astype(jnp.bfloat16)


def draw_store_slot(key, part):
    return storage_order(key)


def draw_passage_ids(key, part):
    storage = storage_order(key)
    key = jax.random.fold_in(key, 3)
    inverse = jnp.argsort(storage, stable=True).astype(jnp.int32)
    picked = jax.vmap(lambda sub: jax.random.permutation(sub, N_DP * PAIR_CAP))(jax.random.split(key, QUESTIONS))
    picked = picked[:, :K_PASS].astype(jnp.int32)
    owners = picked % N_DP
    within = picked // N_DP
    offsets = jax.random.randint(jax.random.fold_in(key, 5), (QUESTIONS, N_DP), 0, P_DEV).astype(jnp.int32)
    start_row = jnp.take_along_axis(offsets, owners, axis=1)
    local_row = (start_row + within) % P_DEV
    return inverse[owners * P_DEV + local_row].astype(jnp.int32)


def draw_lengths(key, part):
    key = jax.random.fold_in(key, 4)
    span = jax.random.randint(key, (PASSAGES,), 2 * PLEN // 3, PLEN + 1).astype(jnp.int32)
    chosen = jax.random.permutation(jax.random.fold_in(key, 7), PASSAGES)
    index_of_row = jnp.arange(PASSAGES)
    span = jnp.where(index_of_row == chosen[0], PLEN, span)
    span = jnp.where(index_of_row == chosen[1], 2 * PLEN // 3, span)
    return span.astype(jnp.int32)


def levels(own_key, extent, shards, low, top_value):
    level = 1.0
    for dim, parts in shards:
        heights = jax.random.uniform(jax.random.fold_in(jax.random.fold_in(own_key, 6), dim), (parts,), jnp.float32, low / len(shards), top_value / len(shards))
        level = level * jnp.repeat(jnp.exp(heights), extent[dim] // parts).reshape((-1,) + (1,) * (len(extent) - 1 - dim))
    return level


def bell_draw(key, extent, width, most, cuts=(), held_as=jnp.bfloat16):
    values = width * jax.random.normal(key, extent, jnp.float32)
    if cuts:
        values = values * levels(key, extent, cuts, -0.22, 0.18)
    return jnp.clip(values, -most, most).astype(held_as)


def setup_inputs(seed: int = 0) -> dict:
    key_of = jax.random.split(jax.random.key(seed), 8)
    return {
        "queries": draw_queries(jax.random.fold_in(key_of[7], 71), 0),
        "keys": draw_keys(jax.random.fold_in(key_of[7], 71), 0),
        "values": bell_draw(key_of[2], (PASSAGES, PLEN, D), 1.0, 6.0, ((0, 32), (2, 16))),
        "cotangent": bell_draw(key_of[3], (QUESTIONS, TGT, D), 32.0, 192.0, ((0, 32), (2, 16))),
        "passage_ids": draw_passage_ids(jax.random.fold_in(key_of[7], 71), 0),
        "store_slot": draw_store_slot(jax.random.fold_in(key_of[7], 71), 0),
        "lengths": draw_lengths(jax.random.fold_in(key_of[7], 71), 0),
    }


score_scale = 0.125


def heads_first(stacked, head_count):
    return stacked.reshape(stacked.shape[0], head_count, -1).transpose(1, 0, 2)


def rows_back(stacked):
    return stacked.transpose(1, 0, 2).reshape(stacked.shape[1], -1)


def head_attention(query_head, key_head, value_head, grad_head, live_keys):
    scores = jnp.dot(query_head, key_head.T, preferred_element_type=jnp.float32) * score_scale
    scores = jnp.where(live_keys[None, :], scores, jnp.float32(-1e30))
    row_max = jnp.max(scores, axis=1, keepdims=True)
    raised = jnp.exp(scores - row_max)
    row_sum = jnp.sum(raised, axis=1, keepdims=True)
    attention_prob = raised / row_sum
    attention_low = attention_prob.astype(jnp.bfloat16)
    context = jnp.dot(attention_low, value_head, preferred_element_type=jnp.float32)
    grad_prob = jnp.dot(grad_head, value_head.T, preferred_element_type=jnp.float32)
    row_delta = jnp.sum(attention_prob * grad_prob, axis=1, keepdims=True)
    grad_scores = (attention_prob * (grad_prob - row_delta)).astype(jnp.bfloat16)
    grad_query = jnp.dot(grad_scores, key_head, preferred_element_type=jnp.float32) * score_scale
    key_gradient = jnp.dot(grad_scores.T, query_head, preferred_element_type=jnp.float32) * score_scale
    grad_value = jnp.dot(attention_low.T, grad_head, preferred_element_type=jnp.float32)
    attention_mass = jnp.sum(attention_prob, axis=0)
    return context, grad_query, key_gradient, grad_value, attention_mass


def reference(queries, keys, values, cotangent, passage_ids, store_slot, lengths):
    position = store_slot[passage_ids]
    list_length = lengths[passage_ids]
    live_table = jnp.arange(PLEN, dtype=jnp.int32)[None, None, :] < list_length[:, :, None]

    def one_question(running, element):
        sum_keys, sum_values, sum_mass = running
        query_rows, grad_rows, slot_rows, live_rows = element
        key_rows = keys[slot_rows].reshape(K_PASS * PLEN, D)
        value_rows = values[slot_rows].reshape(K_PASS * PLEN, D)
        live_keys = live_rows.reshape(K_PASS * PLEN)
        results = lax.map(lambda operands: head_attention(operands[0], operands[1], operands[2], operands[3], live_keys),
                          (heads_first(query_rows, HEADS), heads_first(key_rows, HEADS),
                           heads_first(value_rows, HEADS), heads_first(grad_rows, HEADS)))
        context, grad_query, key_gradient, grad_value, attention_mass = results
        context = rows_back(context).astype(jnp.bfloat16)
        grad_query = rows_back(grad_query).astype(jnp.bfloat16)
        key_grads = rows_back(key_gradient).astype(jnp.bfloat16).reshape(K_PASS, PLEN, D)
        value_grads = rows_back(grad_value).astype(jnp.bfloat16).reshape(K_PASS, PLEN, D)
        passage_mass = (jnp.sum(attention_mass, axis=0).reshape(K_PASS, PLEN).sum(axis=1) / (TGT * HEADS)).astype(jnp.bfloat16)
        passage_mass = lax.optimization_barrier(passage_mass)
        sum_keys = sum_keys.at[slot_rows].add(key_grads.astype(jnp.float32))
        sum_values = sum_values.at[slot_rows].add(value_grads.astype(jnp.float32))
        sum_mass = sum_mass.at[slot_rows].add(passage_mass.astype(jnp.float32))
        return (sum_keys, sum_values, sum_mass), (context, grad_query)

    initial = (jnp.zeros((PASSAGES, PLEN, D), jnp.float32), jnp.zeros((PASSAGES, PLEN, D), jnp.float32),
               jnp.zeros((PASSAGES,), jnp.float32))
    finals, outputs = lax.scan(one_question, initial, (queries, cotangent, position, live_table))
    sum_keys, sum_values, sum_mass = finals
    context, grad_queries = outputs
    return context, grad_queries, sum_keys.astype(jnp.bfloat16), sum_values.astype(jnp.bfloat16), sum_mass
```

```python
import jax
import jax.numpy as jnp
from jax import lax
from jax.experimental import pallas as pl
from jax.experimental.pallas import tpu as pltpu
from jax.sharding import PartitionSpec as P

HD = 64
SCALE = 0.125
NEG = -1e30


def dot_nt(a, b):
    return lax.dot_general(a, b, (((1,), (1,)), ((), ())), preferred_element_type=jnp.float32)


def dot_nn(a, b):
    return lax.dot_general(a, b, (((1,), (0,)), ((), ())), preferred_element_type=jnp.float32)


def pass_one(slot_ref, len_ref, q_ref, g_ref, km_ref, vm_ref, st_ref):
    step = pl.program_id(0)
    live_len = len_ref[step]
    heads = km_ref.shape[1]
    rows = km_ref.shape[2]

    @pl.when(live_len == 0)
    def _():
        st_ref[0, 0] = jnp.full(st_ref.shape[2:], NEG, jnp.float32)
        st_ref[0, 1] = jnp.zeros(st_ref.shape[2:], jnp.float32)
        st_ref[0, 2] = jnp.zeros(st_ref.shape[2:], jnp.float32)

    @pl.when(live_len > 0)
    def _():
        slot = slot_ref[step]
        queries = q_ref[0]
        grads = g_ref[0]
        live = lax.broadcasted_iota(jnp.int32, (rows, queries.shape[0]), 0) < live_len
        for h in range(heads):
            scores = dot_nt(km_ref[slot, h], queries) * SCALE
            scores = jnp.where(live, scores, NEG)
            top = jnp.max(scores, axis=0, keepdims=True)
            raised = jnp.exp(scores - top)
            grad_prob = dot_nt(vm_ref[slot, h], grads)
            st_ref[0, 0, h : h + 1] = top
            st_ref[0, 1, h : h + 1] = jnp.sum(raised, axis=0, keepdims=True)
            st_ref[0, 2, h : h + 1] = jnp.sum(raised * grad_prob, axis=0, keepdims=True)


def pick_heads(stacked, lane):
    heads = len(stacked)
    out = stacked[heads - 1]
    for h in range(heads - 2, -1, -1):
        out = jnp.where(lane < (h + 1) * HD, stacked[h], out)
    return out


def pass_two(
    slot_ref, len_ref, q_ref, g_ref, km_ref, vm_ref, kt_ref, vt_ref, fin_ref,
    o_ref, dq_ref, dk_ref, dv_ref, dk_acc, dv_acc,
):
    step = pl.program_id(0)
    live_len = len_ref[step]
    heads = km_ref.shape[1]
    rows = km_ref.shape[2]

    @pl.when(step == 0)
    def _():
        dk_acc[...] = jnp.zeros_like(dk_acc)
        dv_acc[...] = jnp.zeros_like(dv_acc)

    @pl.when(live_len == 0)
    def _():
        o_ref[...] = jnp.zeros_like(o_ref)
        dq_ref[...] = jnp.zeros_like(dq_ref)

    @pl.when(live_len > 0)
    def _():
        slot = slot_ref[step]
        queries = q_ref[0]
        grads = g_ref[0]
        live = lax.broadcasted_iota(jnp.int32, (rows, queries.shape[0]), 0) < live_len
        lane = lax.broadcasted_iota(jnp.int32, (rows, queries.shape[1]), 1)
        dks, dvs = [], []
        for h in range(heads):
            scores = dot_nt(km_ref[slot, h], queries) * SCALE
            prob = jnp.where(live, jnp.exp(scores - fin_ref[0, 0, h : h + 1]), 0.0)
            low = prob.astype(jnp.bfloat16)
            grad_prob = dot_nt(vm_ref[slot, h], grads)
            gs = (prob * (grad_prob - fin_ref[0, 1, h : h + 1])).astype(jnp.bfloat16)
            cut = slice(h * HD, (h + 1) * HD)
            o_ref[0, cut, :] = dot_nn(vt_ref[slot, cut, :], low)
            dq_ref[0, cut, :] = dot_nn(kt_ref[slot, cut, :], gs)
            dks.append(dot_nn(gs, queries))
            dvs.append(dot_nn(low, grads))
        dk = (pick_heads(dks, lane) * SCALE).astype(jnp.bfloat16)
        dv = pick_heads(dvs, lane).astype(jnp.bfloat16)
        dk_acc[slot] += dk.astype(jnp.float32)
        dv_acc[slot] += dv.astype(jnp.float32)

    @pl.when(step == pl.num_programs(0) - 1)
    def _():
        dk_ref[...] = dk_acc[...].astype(jnp.bfloat16)
        dv_ref[...] = dv_acc[...].astype(jnp.bfloat16)


def local(queries, keys, values, cotangent, passage_ids, store_slot, lengths):
    own = lax.axis_index("dp")
    held, rows, feats = keys.shape
    questions = passage_ids.shape[0]
    target = queries.shape[1]
    heads = feats // HD
    total_heads = heads * lax.axis_size("tensor")
    places = own * held + jnp.arange(held, dtype=jnp.int32)
    match = (store_slot[None, :] == places[:, None]).astype(jnp.int32)
    held_id = jnp.sum(match * jnp.arange(store_slot.shape[0], dtype=jnp.int32)[None, :], axis=1)
    held_len = jnp.sum(match * lengths[None, :], axis=1)
    used = jnp.any(passage_ids[:, :, None] == held_id[None, None, :], axis=1).astype(jnp.int32)
    slot = jnp.sum(used * jnp.arange(held, dtype=jnp.int32)[None, :], axis=1)
    live_len = jnp.sum(used * held_len[None, :], axis=1)

    all_q = lax.all_gather(queries[0], "dp")
    all_g = lax.all_gather(cotangent[0], "dp")

    head_of = jnp.arange(feats, dtype=jnp.int32) // HD
    head_mask = head_of[None, :] == jnp.arange(heads, dtype=jnp.int32)[:, None]
    km = jnp.where(head_mask[None, :, None, :], keys[:, None], jnp.bfloat16(0))
    vm = jnp.where(head_mask[None, :, None, :], values[:, None], jnp.bfloat16(0))
    kt = keys.transpose(0, 2, 1)
    vt = values.transpose(0, 2, 1)

    per_q = lambda *rest: pl.BlockSpec((1,) + rest, lambda i, *_: (i,) + (0,) * len(rest))
    whole = lambda a: pl.BlockSpec(a.shape, lambda i, *_: (0,) * a.ndim)
    stats = pl.pallas_call(
        pass_one,
        grid_spec=pltpu.PrefetchScalarGridSpec(
            num_scalar_prefetch=2,
            grid=(questions,),
            in_specs=[per_q(target, feats), per_q(target, feats), whole(km), whole(vm)],
            out_specs=per_q(3, heads, target),
        ),
        out_shape=jax.ShapeDtypeStruct((questions, 3, heads, target), jnp.float32),
        compiler_params=pltpu.CompilerParams(vmem_limit_bytes=40 << 20),
    )(slot, live_len, all_q, all_g, km, vm)

    got = lax.all_to_all(stats, "dp", split_axis=0, concat_axis=0, tiled=True)
    top = jnp.max(got[:, 0], axis=0)
    weight = jnp.exp(got[:, 0] - top[None])
    total = jnp.sum(got[:, 1] * weight, axis=0)
    delta = jnp.sum(got[:, 2] * weight, axis=0) / total
    final = jnp.stack([top + jnp.log(total), delta])
    fin = lax.all_gather(final, "dp")

    out_t = jax.ShapeDtypeStruct((questions, feats, target), jnp.float32)
    o_t, dq_t, dk, dv = pl.pallas_call(
        pass_two,
        grid_spec=pltpu.PrefetchScalarGridSpec(
            num_scalar_prefetch=2,
            grid=(questions,),
            in_specs=[per_q(target, feats), per_q(target, feats), whole(km), whole(vm),
                      whole(kt), whole(vt), per_q(2, heads, target)],
            out_specs=[per_q(feats, target), per_q(feats, target), whole(keys), whole(values)],
            scratch_shapes=[pltpu.VMEM(keys.shape, jnp.float32), pltpu.VMEM(values.shape, jnp.float32)],
        ),
        out_shape=[out_t, out_t, jax.ShapeDtypeStruct(keys.shape, keys.dtype),
                   jax.ShapeDtypeStruct(values.shape, values.dtype)],
        compiler_params=pltpu.CompilerParams(vmem_limit_bytes=48 << 20),
    )(slot, live_len, all_q, all_g, km, vm, kt, vt, fin)

    mass = jnp.sum(stats[:, 1] * jnp.exp(stats[:, 0] - fin[:, 0]), axis=(1, 2)) / (target * total_heads)
    mass = lax.psum(mass, "tensor").astype(jnp.bfloat16).astype(jnp.float32)
    relevance = jnp.sum(used.astype(jnp.float32) * mass[:, None], axis=0)

    o_sum = lax.psum_scatter(o_t, "dp", scatter_dimension=0, tiled=True)
    dq_sum = lax.psum_scatter(dq_t, "dp", scatter_dimension=0, tiled=True)
    context = o_sum.transpose(0, 2, 1).astype(jnp.bfloat16)
    grad_queries = (dq_sum.transpose(0, 2, 1) * SCALE).astype(jnp.bfloat16)
    return context, grad_queries, dk, dv, relevance


def solution(mesh):
    wide = P("dp", None, "tensor")
    return jax.shard_map(
        local,
        mesh=mesh,
        in_specs=(wide, wide, wide, wide, P(), P(), P()),
        out_specs=(wide, wide, wide, wide, P("dp")),
        check_vma=False,
    )
```

```python
import functools

import jax
import jax.numpy as jnp
from jax import lax
from jax.experimental import pallas as pl
from jax.experimental.pallas import tpu as pltpu
from jax.sharding import PartitionSpec as P

HD = 64
SCALE = 0.125
NEG = -1e30
NX = 4
LAG = 2
STEPS = ((1, 0), (-1, 0), (0, 1), (0, -1))


def onward(kind, dy, dx, ny, nx):
    def along(near, size, plus_reach, plus_link):
        links = []
        minus_reach = size - 1 - plus_reach
        gone_plus, gone_minus = (-near) % size, near % size
        if gone_plus < plus_reach:
            links.append(plus_link)
        if gone_minus < minus_reach and (gone_plus == 0 or gone_plus > plus_reach):
            links.append(plus_link + 1)
        return links

    if kind == 0:
        links = along(dx, nx, nx // 2 if dy % 2 == 0 else nx - 1 - nx // 2, 2)
        if dx == 0:
            links += along(dy, ny, ny // 2, 0)
    else:
        links = along(dy, ny, ny // 2 if dx % 2 == 0 else ny - 1 - ny // 2, 0)
        if dx == 0 or dy == 0:
            pass
        if dy == 0:
            links += along(dx, nx, nx - 1 - nx // 2, 2)
    return links


@functools.lru_cache(maxsize=None)
def schedule(ny, nx):
    def moved(link, dy, dx):
        return ((dy - STEPS[link][0]) % ny, (dx - STEPS[link][1]) % nx)

    @functools.lru_cache(maxsize=None)
    def height(kind, dy, dx, link):
        to = moved(link, dy, dx)
        return 1 + max([height(kind, *to, n) for n in onward(kind, *to, ny, nx)], default=0)

    came = {(0, 0, 0): -LAG, (1, 0, 0): -LAG}
    todo = {(k, 0, 0, n) for k in (0, 1) for n in onward(k, 0, 0, ny, nx)}
    slots = []
    while todo:
        t = len(slots)
        now, fresh = [], {}
        for link in range(4):
            able = [j for j in todo if j[3] == link and came[j[:3]] <= t - LAG]
            if able:
                best = max(able, key=lambda j: (height(*j), j))
                todo.remove(best)
                to = moved(link, best[1], best[2])
                now.append((link, best[0], best[1:3], to))
                fresh[(best[0],) + to] = t
        came.update(fresh)
        for k, dy, dx in fresh:
            todo |= {(k, dy, dx, n) for n in onward(k, dy, dx, ny, nx)}
        slots.append(now)
    places = [(dy, dx) for dy in range(ny) for dx in range(nx)]
    ready = {p: max(came[(0,) + p], came[(1,) + p]) for p in places}
    order = sorted(places, key=lambda p: (ready[p], p))
    return slots, order, ready


def dot_nt(a, b):
    return lax.dot_general(a, b, (((1,), (1,)), ((), ())), preferred_element_type=jnp.float32)


def dot_nn(a, b):
    return lax.dot_general(a, b, (((1,), (0,)), ((), ())), preferred_element_type=jnp.float32)


def peer(ny, nx, dy, dx):
    own = lax.axis_index("dp")
    y, x = own // nx, own % nx
    return {"dp": ((y + dy) % ny) * nx + (x + dx) % nx}


def greet(ny, nx, offsets):
    barrier = pltpu.get_barrier_semaphore()
    for off in offsets:
        pl.semaphore_signal(barrier, inc=1, device_id=peer(ny, nx, *off), device_id_type=pl.DeviceIdType.MESH)
    pl.semaphore_wait(barrier, len(offsets))


def gather_kernel(ny, nx, slot_ref, len_ref, q_ref, g_ref, km_ref, vm_ref, aq_ref, ag_ref, st_ref, send_sem, recv_sem):
    slots, order, ready = schedule(ny, nx)
    index = {p: i for i, p in enumerate(order)}
    bufs = (aq_ref, ag_ref)
    count = ny * nx
    rows = km_ref.shape[1] // (km_ref.shape[2] // HD)
    heads = km_ref.shape[2] // HD

    def copies(t):
        out = []
        for link, kind, sent, got in slots[t]:
            out.append(
                pltpu.make_async_remote_copy(
                    src_ref=bufs[kind].at[index[sent]],
                    dst_ref=bufs[kind].at[index[got]],
                    send_sem=send_sem.at[t, link],
                    recv_sem=recv_sem.at[t, link],
                    device_id=peer(ny, nx, *STEPS[link]),
                    device_id_type=pl.DeviceIdType.MESH,
                )
            )
        return out

    def advance(t):
        if t >= LAG:
            for copy in copies(t - LAG):
                copy.wait_recv()
        if t < len(slots):
            for copy in copies(t):
                copy.start()

    aq_ref[0] = q_ref[0]
    ag_ref[0] = g_ref[0]
    greet(ny, nx, STEPS)

    live_row = lax.broadcasted_iota(jnp.int32, (rows, q_ref.shape[1]), 0)

    def body(i, carry):
        passed = 0
        for c in range(count):
            upto = len(slots) + LAG if c == count - 1 else max(passed, ready[order[c]] + LAG + 1)
            if upto > passed:

                @pl.when(i == c)
                def _():
                    for t in range(passed, upto):
                        advance(t)

                passed = upto
        slot = slot_ref[i]
        live = live_row < len_ref[i]
        all_scores = dot_nt(km_ref[slot], aq_ref[i])
        all_grads = dot_nt(vm_ref[slot], ag_ref[i])
        for h in range(heads):
            part = slice(h * rows, (h + 1) * rows)
            scores = jnp.where(live, all_scores[part], NEG)
            top = jnp.max(scores, axis=0, keepdims=True)
            raised = jnp.exp(scores - top)
            st_ref[i, h : h + 1] = top
            st_ref[i, heads + h : heads + h + 1] = jnp.sum(raised, axis=0, keepdims=True)
            st_ref[i, 2 * heads + h : 2 * heads + h + 1] = jnp.sum(raised * all_grads[part], axis=0, keepdims=True)
        return carry

    lax.fori_loop(0, count, body, 0)
    for t in range(len(slots)):
        for copy in copies(t):
            copy.wait_send()


def stats_kernel(ny, nx, st_ref, fin_ref, got, send_sem, recv_sem, send_two, recv_two):
    _, order, _ = schedule(ny, nx)
    index = {p: i for i, p in enumerate(order)}
    heads = st_ref.shape[1] // 3
    greet(ny, nx, order[1:])
    there, back = [], []
    for i, off in enumerate(order[1:], 1):
        there.append(
            pltpu.make_async_remote_copy(
                src_ref=st_ref.at[i], dst_ref=got.at[i], send_sem=send_sem.at[i], recv_sem=recv_sem.at[i],
                device_id=peer(ny, nx, *off), device_id_type=pl.DeviceIdType.MESH,
            )
        )
        mirror = index[((-off[0]) % ny, (-off[1]) % nx)]
        back.append(
            pltpu.make_async_remote_copy(
                src_ref=fin_ref.at[0], dst_ref=fin_ref.at[mirror], send_sem=send_two.at[i], recv_sem=recv_two.at[i],
                device_id=peer(ny, nx, *off), device_id_type=pl.DeviceIdType.MESH,
            )
        )
    for copy in there:
        copy.start()
    got[0] = st_ref[0]
    for copy in there:
        copy.wait_recv()
    tops = got[:, :heads, :]
    top = jnp.max(tops, axis=0)
    weight = jnp.exp(tops - top[None])
    total = jnp.sum(got[:, heads : 2 * heads, :] * weight, axis=0)
    delta = jnp.sum(got[:, 2 * heads :, :] * weight, axis=0) / total
    fin_ref[0, :heads] = top + jnp.log(total)
    fin_ref[0, heads:] = delta
    for copy in back:
        copy.start()
    for copy in back:
        copy.wait_recv()
    for copy in there + back:
        copy.wait_send()


def pick_heads(stacked, lane):
    heads = len(stacked)
    out = stacked[heads - 1]
    for h in range(heads - 2, -1, -1):
        out = jnp.where(lane < (h + 1) * HD, stacked[h], out)
    return out


def reduce_kernel(
    ny, nx, slot_ref, len_ref, aq_ref, ag_ref, km_ref, vm_ref, kt_ref, vt_ref, fin_ref,
    ctx_ref, gq_ref, dk_ref, dv_ref, own_o, own_q, sent_buf, got_buf, dk_acc, dv_acc, send_sem, recv_sem,
):
    slots, order, _ = schedule(ny, nx)
    index = {p: i for i, p in enumerate(order)}
    count = ny * nx
    last = len(slots) - 1
    feats, target = kt_ref.shape[1], aq_ref.shape[1]
    heads = feats // HD
    rows = kt_ref.shape[2]
    held = kt_ref.shape[0]
    owns = (own_o, own_q)
    entries = [(t,) + e for t in range(len(slots)) for e in slots[t]]

    def copy_of(n):
        _, link, _, _, _ = entries[n]
        back = (-STEPS[link][0], -STEPS[link][1])
        return pltpu.make_async_remote_copy(
            src_ref=sent_buf.at[n], dst_ref=got_buf.at[n], send_sem=send_sem.at[n], recv_sem=recv_sem.at[n],
            device_id=peer(ny, nx, *back), device_id_type=pl.DeviceIdType.MESH,
        )

    def children(kind, place):
        return [n for n, (_, _, k, sent, _) in enumerate(entries) if k == kind and sent == place]

    def summed(kind, place):
        kids = children(kind, place)
        for n in kids:
            copy_of(n).wait_recv()
        powers = [jnp.exp2(got_buf[n, feats : feats + 16, :].astype(jnp.float32)) for n in kids]
        for h in range(heads):
            cut = slice(h * HD, (h + 1) * HD)
            acc = owns[kind][index[place], cut, :]
            for n, power in zip(kids, powers):
                acc = acc + got_buf[n, cut, :].astype(jnp.float32) * power[h : h + 1]
            yield cut, acc

    row16 = lax.broadcasted_iota(jnp.int32, (16, target), 0)

    def send_on(n):
        _, _, kind, _, place = entries[n]
        shifts = jnp.zeros((16, target), jnp.float32)
        for h, (cut, acc) in enumerate(summed(kind, place)):
            most = jnp.maximum(jnp.max(jnp.abs(acc), axis=0, keepdims=True), 1e-30)
            shift = jnp.ceil(jnp.log2(most) + 0.01) - 15.0
            coded = jnp.floor(acc * jnp.exp2(-shift) + 0.5)
            sent_buf[n, cut, :] = coded.astype(jnp.int32).astype(jnp.int16)
            shifts = jnp.where(row16 == h, shift, shifts)
        sent_buf[n, feats : feats + 16, :] = shifts.astype(jnp.int32).astype(jnp.int16)
        copy_of(n).start()

    dk_acc[...] = jnp.zeros_like(dk_acc)
    dv_acc[...] = jnp.zeros_like(dv_acc)
    greet(ny, nx, STEPS)

    live_row = lax.broadcasted_iota(jnp.int32, (rows, target), 0)
    lane = lax.broadcasted_iota(jnp.int32, (rows, feats), 1)

    def body(step, carry):
        i = count - 1 - step
        slot = slot_ref[i]
        live = live_row < len_ref[i]
        queries = aq_ref[i]
        grads = ag_ref[i]
        all_scores = dot_nt(km_ref[slot], queries)
        all_grads = dot_nt(vm_ref[slot], grads)
        dks, dvs = [], []
        for h in range(heads):
            part = slice(h * rows, (h + 1) * rows)
            cut = slice(h * HD, (h + 1) * HD)
            prob = jnp.where(live, jnp.exp(all_scores[part] - fin_ref[i, h : h + 1]), 0.0)
            low = prob.astype(jnp.bfloat16)
            gs = (prob * (all_grads[part] - fin_ref[i, heads + h : heads + h + 1])).astype(jnp.bfloat16)
            own_o[i, cut, :] = dot_nn(vt_ref[slot, cut, :], low)
            own_q[i, cut, :] = dot_nn(kt_ref[slot, cut, :], gs)
            dks.append(dot_nn(gs, queries))
            dvs.append(dot_nn(low, grads))
        dk = (pick_heads(dks, lane) * SCALE).astype(jnp.bfloat16).astype(jnp.float32)
        dv = pick_heads(dvs, lane).astype(jnp.bfloat16).astype(jnp.float32)
        for s in range(held):
            mine = jnp.where(slot == s, 1.0, 0.0)
            dk_acc[s] += dk * mine
            dv_acc[s] += dv * mine

        passed = 0
        for c in range(count):
            upto = passed
            while upto <= last and all(index[e[3]] >= count - 1 - c for e in slots[last - upto]):
                upto += 1
            if upto > passed:

                @pl.when(step == c)
                def _():
                    for u in range(passed, upto):
                        for n, e in enumerate(entries):
                            if e[0] == last - u:
                                send_on(n)

                passed = upto
        return carry

    lax.fori_loop(0, count, body, 0)
    dk_ref[...] = dk_acc[...].astype(jnp.bfloat16)
    dv_ref[...] = dv_acc[...].astype(jnp.bfloat16)
    for kind, out, factor in ((0, ctx_ref, 1.0), (1, gq_ref, SCALE)):
        whole = jnp.concatenate([acc for _, acc in summed(kind, (0, 0))], axis=0)
        out[0] = (whole.T * factor).astype(jnp.bfloat16)
    for n in range(len(entries)):
        copy_of(n).wait_send()


def local(queries, keys, values, cotangent, passage_ids, store_slot, lengths):
    own = lax.axis_index("dp")
    count = lax.axis_size("dp")
    nx = NX
    ny = count // nx
    slots, order, _ = schedule(ny, nx)
    entry_count = sum(len(s) for s in slots)
    held, rows, feats = keys.shape
    target = queries.shape[1]
    heads = feats // HD
    total_heads = heads * lax.axis_size("tensor")

    dys = jnp.array([p[0] for p in order], jnp.int32)
    dxs = jnp.array([p[1] for p in order], jnp.int32)
    question = ((own // nx + dys) % ny) * nx + (own % nx + dxs) % nx
    places = own * held + jnp.arange(held, dtype=jnp.int32)
    match = (store_slot[None, :] == places[:, None]).astype(jnp.int32)
    held_id = jnp.sum(match * jnp.arange(store_slot.shape[0], dtype=jnp.int32)[None, :], axis=1)
    held_len = jnp.sum(match * lengths[None, :], axis=1)
    hit = jnp.any(passage_ids[:, :, None] == held_id[None, None, :], axis=1)
    turn = question[:, None] == jnp.arange(count, dtype=jnp.int32)[None, :]
    used = jnp.any(turn[:, :, None] & hit[None, :, :], axis=1).astype(jnp.int32)
    slot = jnp.sum(used * jnp.arange(held, dtype=jnp.int32)[None, :], axis=1)
    live_len = jnp.sum(used * held_len[None, :], axis=1)

    head_of = jnp.arange(feats, dtype=jnp.int32) // HD
    head_mask = (head_of[None, :] == jnp.arange(heads, dtype=jnp.int32)[:, None])[None, :, None, :]
    zero = jnp.bfloat16(0)
    km = jnp.where(head_mask, (keys * jnp.bfloat16(SCALE))[:, None], zero).reshape(held, heads * rows, feats)
    vm = jnp.where(head_mask, values[:, None], zero).reshape(held, heads * rows, feats)
    kt = keys.transpose(0, 2, 1)
    vt = values.transpose(0, 2, 1)

    vmem = pl.BlockSpec(memory_space=pltpu.VMEM)
    smem = pl.BlockSpec(memory_space=pltpu.SMEM)
    dma = pltpu.SemaphoreType.DMA
    gathered = jax.ShapeDtypeStruct((count, target, feats), jnp.bfloat16)
    all_q, all_g, stats = pl.pallas_call(
        functools.partial(gather_kernel, ny, nx),
        in_specs=[smem, smem] + [vmem] * 4,
        out_specs=[vmem] * 3,
        out_shape=[gathered, gathered, jax.ShapeDtypeStruct((count, 3 * heads, target), jnp.float32)],
        scratch_shapes=[dma((len(slots), 4)), dma((len(slots), 4))],
        compiler_params=pltpu.CompilerParams(collective_id=0, has_side_effects=True, vmem_limit_bytes=40 << 20),
    )(slot, live_len, queries, cotangent, km, vm)

    fin = pl.pallas_call(
        functools.partial(stats_kernel, ny, nx),
        in_specs=[vmem],
        out_specs=vmem,
        out_shape=jax.ShapeDtypeStruct((count, 2 * heads, target), jnp.float32),
        scratch_shapes=[pltpu.VMEM((count, 3 * heads, target), jnp.float32)] + [dma((count,))] * 4,
        compiler_params=pltpu.CompilerParams(collective_id=1, has_side_effects=True, vmem_limit_bytes=16 << 20),
    )(stats)

    mass = jnp.sum(stats[:, heads : 2 * heads] * jnp.exp(stats[:, :heads] - fin[:, :heads]), axis=(1, 2))
    mass = lax.psum(mass / (target * total_heads), "tensor").astype(jnp.bfloat16).astype(jnp.float32)
    relevance = jnp.sum(used.astype(jnp.float32) * mass[:, None], axis=0)

    context, grad_queries, grad_keys, grad_values = pl.pallas_call(
        functools.partial(reduce_kernel, ny, nx),
        in_specs=[smem, smem] + [vmem] * 7,
        out_specs=[vmem] * 4,
        out_shape=[jax.ShapeDtypeStruct(a.shape, a.dtype) for a in (queries, queries, keys, values)],
        scratch_shapes=[
            pltpu.VMEM((count, feats, target), jnp.float32),
            pltpu.VMEM((count, feats, target), jnp.float32),
            pltpu.VMEM((entry_count, feats + 16, target), jnp.int16),
            pltpu.VMEM((entry_count, feats + 16, target), jnp.int16),
            pltpu.VMEM(keys.shape, jnp.float32),
            pltpu.VMEM(values.shape, jnp.float32),
            dma((entry_count,)),
            dma((entry_count,)),
        ],
        compiler_params=pltpu.CompilerParams(collective_id=2, has_side_effects=True, vmem_limit_bytes=60 << 20),
    )(slot, live_len, all_q, all_g, km, vm, kt, vt, fin)
    return context, grad_queries, grad_keys, grad_values, relevance


def solution(mesh):
    wide = P("dp", None, "tensor")
    return jax.shard_map(
        local,
        mesh=mesh,
        in_specs=(wide, wide, wide, wide, P(), P(), P()),
        out_specs=(wide, wide, wide, wide, P("dp")),
        check_vma=False,
    )
```

```python
import functools

import jax
import jax.numpy as jnp
from jax import lax
from jax.experimental import pallas as pl
from jax.experimental.pallas import tpu as pltpu
from jax.sharding import PartitionSpec as P

HD = 64
SCALE = 0.125
NEG = -1e30
NX = 4
LAG = 2
STEPS = ((1, 0), (-1, 0), (0, 1), (0, -1))


def onward(kind, dy, dx, ny, nx):
    def along(near, size, plus_reach, plus_link):
        links = []
        minus_reach = size - 1 - plus_reach
        gone_plus, gone_minus = (-near) % size, near % size
        if gone_plus < plus_reach:
            links.append(plus_link)
        if gone_minus < minus_reach and (gone_plus == 0 or gone_plus > plus_reach):
            links.append(plus_link + 1)
        return links

    up = ny // 2
    if kind == 0:
        links = along(dx, nx, nx // 2 if dy % 4 != 3 else nx - 1 - nx // 2, 2)
        if dx == 0:
            links += along(dy, ny, up, 0)
        return links
    far = nx // 2
    plus = up if dx % 2 == 0 else ny - 1 - up
    gone_plus, gone_minus = (-dy) % ny, dy % ny
    near_row = gone_plus <= ny // 4 or gone_minus <= (ny - 1 - up) // 2
    links = along(dy, ny, plus, 0)
    if dx == far:
        links = [n for n in links if (gone_plus < ny // 4 if n == 0 else gone_minus < (ny - 1 - up) // 2)]
    if dy == 0:
        links += along(dx, nx, nx - 1 - far, 2)
    elif dx == far - 1 and not near_row:
        links.append(3)
    return links


@functools.lru_cache(maxsize=None)
def schedule(ny, nx):
    def moved(link, dy, dx):
        return ((dy - STEPS[link][0]) % ny, (dx - STEPS[link][1]) % nx)

    @functools.lru_cache(maxsize=None)
    def height(kind, dy, dx, link):
        to = moved(link, dy, dx)
        return 1 + max([height(kind, *to, n) for n in onward(kind, *to, ny, nx)], default=0)

    came = {(0, 0, 0): -LAG, (1, 0, 0): -LAG}
    todo = {(k, 0, 0, n) for k in (0, 1) for n in onward(k, 0, 0, ny, nx)}
    slots = []
    while todo:
        t = len(slots)
        now, fresh = [], {}
        for link in range(4):
            able = [j for j in todo if j[3] == link and came[j[:3]] <= t - LAG]
            if able:
                best = max(able, key=lambda j: (height(*j), j))
                todo.remove(best)
                to = moved(link, best[1], best[2])
                now.append((link, best[0], best[1:3], to))
                fresh[(best[0],) + to] = t
        came.update(fresh)
        for k, dy, dx in fresh:
            todo |= {(k, dy, dx, n) for n in onward(k, dy, dx, ny, nx)}
        slots.append(now)
    places = [(dy, dx) for dy in range(ny) for dx in range(nx)]
    ready = {p: max(came[(0,) + p], came[(1,) + p]) for p in places}
    order = sorted(places, key=lambda p: (ready[p], p))
    return slots, order, ready


def dot_nt(a, b):
    return lax.dot_general(a, b, (((1,), (1,)), ((), ())), preferred_element_type=jnp.float32)


def dot_nn(a, b):
    return lax.dot_general(a, b, (((1,), (0,)), ((), ())), preferred_element_type=jnp.float32)


def peer(ny, nx, dy, dx):
    own = lax.axis_index("dp")
    y, x = own // nx, own % nx
    return {"dp": ((y + dy) % ny) * nx + (x + dx) % nx}


def remote(src, dst, send_sem, recv_sem, device):
    return pltpu.make_async_remote_copy(
        src_ref=src, dst_ref=dst, send_sem=send_sem, recv_sem=recv_sem,
        device_id=device, device_id_type=pl.DeviceIdType.MESH,
    )


def pick_heads(stacked, lane):
    heads = len(stacked)
    out = stacked[heads - 1]
    for h in range(heads - 2, -1, -1):
        out = jnp.where(lane < (h + 1) * HD, stacked[h], out)
    return out


def merged(parts, heads):
    top = parts[0][:heads]
    for part in parts[1:]:
        top = jnp.maximum(top, part[:heads])
    total = delta = 0.0
    for part in parts:
        weight = jnp.exp(part[:heads] - top)
        total = total + part[heads : 2 * heads] * weight
        delta = delta + part[2 * heads :] * weight
    return top, total, delta


def kernel(
    ny, nx, ranks, slot_ref, len_ref, q_ref, g_ref, k_ref, v_ref,
    ctx_ref, gq_ref, dk_ref, dv_ref, mass_ref,
    aq, ag, km, vm, kt, vt, st, got_x, mid, got_y, fin_x, fin, mass_rows, mass_own, mass_got,
    own_o, own_q, sent_buf, got_buf, dk_acc, dv_acc,
    send_sem, recv_sem, sx_sem, rx_sem, sy_sem, ry_sem, sf_sem, rf_sem, sd_sem, rd_sem, sm_sem, rm_sem, sr_sem, rr_sem,
):
    slots, order, ready = schedule(ny, nx)
    index = {p: i for i, p in enumerate(order)}
    count = ny * nx
    last = len(slots) - 1
    held, rows, feats = k_ref.shape
    target = q_ref.shape[1]
    heads = feats // HD
    rank = lax.axis_index("tensor")
    entries = [(t,) + e for t in range(len(slots)) for e in slots[t]]

    aq[0] = q_ref[0]
    ag[0] = g_ref[0]
    barrier = pltpu.get_barrier_semaphore()
    met = [peer(ny, nx, 0, dx) for dx in range(1, nx)] + [peer(ny, nx, dy, 0) for dy in range(1, ny)]
    met += [{"tensor": lax.rem(rank + r, ranks)} for r in range(1, ranks)]
    for device in met:
        pl.semaphore_signal(barrier, inc=1, device_id=device, device_id_type=pl.DeviceIdType.MESH)
    pl.semaphore_wait(barrier, len(met))

    def gathers(t):
        return [
            remote((aq, ag)[kind].at[index[sent]], (aq, ag)[kind].at[index[got]], send_sem.at[t, link],
                   recv_sem.at[t, link], peer(ny, nx, *STEPS[link]))
            for link, kind, sent, got in slots[t]
        ]

    def advance(t):
        if t >= LAG:
            for copy in gathers(t - LAG):
                copy.wait_recv()
        if t < len(slots):
            for copy in gathers(t):
                copy.start()

    def stat_x(i):
        dy, dx = order[i]
        return remote(st.at[i], got_x.at[dy, (-dx) % nx], sx_sem.at[dy, dx], rx_sem.at[dy, (-dx) % nx], peer(ny, nx, 0, dx))

    first = ready[order[0]] + LAG + 1
    for t in range(first):
        advance(t)

    lane = lax.broadcasted_iota(jnp.int32, (rows, feats), 1)
    for s in range(held):
        keys, values = k_ref[s], v_ref[s]
        kt[s] = keys.astype(jnp.float32).T.astype(jnp.bfloat16)
        vt[s] = values.astype(jnp.float32).T.astype(jnp.bfloat16)
        for h in range(heads):
            mine = (lane >= h * HD) & (lane < (h + 1) * HD)
            km[s, h * rows : (h + 1) * rows] = jnp.where(mine, keys.astype(jnp.float32) * SCALE, 0.0).astype(jnp.bfloat16)
            vm[s, h * rows : (h + 1) * rows] = jnp.where(mine, values.astype(jnp.float32), 0.0).astype(jnp.bfloat16)

    live_row = lax.broadcasted_iota(jnp.int32, (rows, target), 0)

    def pass_one(i, carry):
        passed = first
        for c in range(1, count):
            upto = len(slots) + LAG if c == count - 1 else max(passed, ready[order[c]] + LAG + 1)

            @pl.when(i == c)
            def _():
                for t in range(passed, upto):
                    advance(t)
                if order[c - 1][1]:
                    stat_x(c - 1).start()

            passed = upto
        slot = slot_ref[i]
        live = live_row < len_ref[i]
        all_scores = dot_nt(km[slot], aq[i])
        all_grads = dot_nt(vm[slot], ag[i])
        for h in range(heads):
            part = slice(h * rows, (h + 1) * rows)
            scores = jnp.where(live, all_scores[part], NEG)
            top = jnp.max(scores, axis=0, keepdims=True)
            raised = jnp.exp(scores - top)
            st[i, h : h + 1] = top
            st[i, heads + h : heads + h + 1] = jnp.sum(raised, axis=0, keepdims=True)
            st[i, 2 * heads + h : 2 * heads + h + 1] = jnp.sum(raised * all_grads[part], axis=0, keepdims=True)
        return carry

    lax.fori_loop(0, count, pass_one, 0)
    if order[count - 1][1]:
        stat_x(count - 1).start()

    def stat_y(dy):
        return remote(mid.at[dy], got_y.at[(-dy) % ny], sy_sem.at[dy], ry_sem.at[(-dy) % ny], peer(ny, nx, dy, 0))

    def fin_y(dy):
        return remote(fin_x.at[0, 0], fin_x.at[0, (-dy) % ny], sf_sem.at[dy], rf_sem.at[(-dy) % ny], peer(ny, nx, dy, 0))

    def fin_over_x(dx):
        return remote(fin_x.at[0], fin_x.at[(-dx) % nx], sd_sem.at[dx], rd_sem.at[(-dx) % nx], peer(ny, nx, 0, dx))

    for dy in list(range(1, ny)) + [0]:
        for dx in range(1, nx):
            stat_x(index[(dy, (-dx) % nx)]).wait_recv()
        parts = [st[index[(dy, 0)]]] + [got_x[dy, dx] for dx in range(1, nx)]
        for n, part in enumerate(merged(parts, heads)):
            mid[dy, n * heads : (n + 1) * heads] = part
        if dy:
            stat_y(dy).start()
    for dy in range(1, ny):
        stat_y((-dy) % ny).wait_recv()
    top, total, delta = merged([mid[0]] + [got_y[dy] for dy in range(1, ny)], heads)
    fin_x[0, 0, :heads] = top + jnp.log(total)
    fin_x[0, 0, heads:] = delta / total
    for dy in range(1, ny):
        fin_y(dy).start()
    for dy in range(1, ny):
        fin_y((-dy) % ny).wait_recv()
    for dx in range(1, nx):
        fin_over_x(dx).start()
    for dx in range(1, nx):
        fin_over_x((-dx) % nx).wait_recv()
    for i, (dy, dx) in enumerate(order):
        fin[i] = fin_x[dx, dy]
        share = st[i, heads : 2 * heads] * jnp.exp(st[i, :heads] - fin[i, :heads])
        mass_rows[i : i + 1] = jnp.sum(share, axis=0, keepdims=True)
    mass_own[...] = jnp.broadcast_to(jnp.sum(mass_rows[...], axis=1, keepdims=True), mass_own.shape)

    def masses(r):
        return remote(mass_own, mass_got.at[r], sm_sem.at[r], rm_sem.at[r], {"tensor": lax.rem(rank + r, ranks)})

    for r in range(1, ranks):
        masses(r).start()

    owns = (own_o, own_q)

    def copy_of(n):
        link = entries[n][1]
        return remote(sent_buf.at[n], got_buf.at[n], sr_sem.at[n], rr_sem.at[n], peer(ny, nx, -STEPS[link][0], -STEPS[link][1]))

    def summed(kind, place):
        kids = [n for n, (_, _, k, sent, _) in enumerate(entries) if k == kind and sent == place]
        for n in kids:
            copy_of(n).wait_recv()
        powers = [jnp.exp2(got_buf[n, feats : feats + 16, :].astype(jnp.float32)) for n in kids]
        for h in range(heads):
            cut = slice(h * HD, (h + 1) * HD)
            acc = owns[kind][index[place], cut, :]
            for n, power in zip(kids, powers):
                acc = acc + got_buf[n, cut, :].astype(jnp.float32) * power[h : h + 1]
            yield cut, acc

    row16 = lax.broadcasted_iota(jnp.int32, (16, target), 0)

    def send_on(n):
        _, _, kind, _, place = entries[n]
        shifts = jnp.zeros((16, target), jnp.float32)
        for h, (cut, acc) in enumerate(summed(kind, place)):
            most = jnp.maximum(jnp.max(jnp.abs(acc), axis=0, keepdims=True), 1e-30)
            shift = jnp.ceil(jnp.log2(most) + 0.01) - 15.0
            coded = jnp.floor(acc * jnp.exp2(-shift) + 0.5)
            sent_buf[n, cut, :] = coded.astype(jnp.int32).astype(jnp.int16)
            shifts = jnp.where(row16 == h, shift, shifts)
        sent_buf[n, feats : feats + 16, :] = shifts.astype(jnp.int32).astype(jnp.int16)
        copy_of(n).start()

    dk_acc[...] = jnp.zeros_like(dk_acc)
    dv_acc[...] = jnp.zeros_like(dv_acc)

    def pass_two(step, carry):
        i = count - 1 - step
        slot = slot_ref[i]
        live = live_row < len_ref[i]
        queries = aq[i]
        grads = ag[i]
        all_scores = dot_nt(km[slot], queries)
        all_grads = dot_nt(vm[slot], grads)
        dks, dvs = [], []
        for h in range(heads):
            part = slice(h * rows, (h + 1) * rows)
            cut = slice(h * HD, (h + 1) * HD)
            prob = jnp.where(live, jnp.exp(all_scores[part] - fin[i, h : h + 1]), 0.0)
            low = prob.astype(jnp.bfloat16)
            gs = (prob * (all_grads[part] - fin[i, heads + h : heads + h + 1])).astype(jnp.bfloat16)
            own_o[i, cut, :] = dot_nn(vt[slot, cut, :], low)
            own_q[i, cut, :] = dot_nn(kt[slot, cut, :], gs)
            dks.append(dot_nn(gs, queries))
            dvs.append(dot_nn(low, grads))
        dk = (pick_heads(dks, lane) * SCALE).astype(jnp.bfloat16).astype(jnp.float32)
        dv = pick_heads(dvs, lane).astype(jnp.bfloat16).astype(jnp.float32)
        for s in range(held):
            mine = jnp.where(slot == s, 1.0, 0.0)
            dk_acc[s] += dk * mine
            dv_acc[s] += dv * mine

        passed = 0
        for c in range(count):
            upto = passed
            while upto <= last and all(index[e[3]] >= count - 1 - c for e in slots[last - upto]):
                upto += 1
            if upto > passed:

                @pl.when(step == c)
                def _():
                    for u in range(passed, upto):
                        for n, e in enumerate(entries):
                            if e[0] == last - u:
                                send_on(n)

                passed = upto
        return carry

    lax.fori_loop(0, count, pass_two, 0)
    dk_ref[...] = dk_acc[...].astype(jnp.bfloat16)
    dv_ref[...] = dv_acc[...].astype(jnp.bfloat16)
    mass = mass_own[...]
    for r in range(1, ranks):
        masses(r).wait_recv()
        mass = mass + mass_got[r]
    mass_ref[...] = (mass / (target * heads * ranks)).astype(jnp.bfloat16).astype(jnp.float32)
    for kind, out, factor in ((0, ctx_ref, 1.0), (1, gq_ref, SCALE)):
        whole = jnp.concatenate([acc for _, acc in summed(kind, (0, 0))], axis=0)
        out[0] = (whole.T * factor).astype(jnp.bfloat16)

    for t in range(len(slots)):
        for copy in gathers(t):
            copy.wait_send()
    for i in range(count):
        if order[i][1]:
            stat_x(i).wait_send()
    for dy in range(1, ny):
        stat_y(dy).wait_send()
        fin_y(dy).wait_send()
    for dx in range(1, nx):
        fin_over_x(dx).wait_send()
    for r in range(1, ranks):
        masses(r).wait_send()
    for n in range(len(entries)):
        copy_of(n).wait_send()


def local(queries, keys, values, cotangent, passage_ids, store_slot, lengths):
    own = lax.axis_index("dp")
    count = lax.axis_size("dp")
    nx = NX
    ny = count // nx
    slots, order, _ = schedule(ny, nx)
    entry_count = sum(len(s) for s in slots)
    held, rows, feats = keys.shape
    target = queries.shape[1]
    heads = feats // HD

    dys = jnp.array([p[0] for p in order], jnp.int32)
    dxs = jnp.array([p[1] for p in order], jnp.int32)
    question = ((own // nx + dys) % ny) * nx + (own % nx + dxs) % nx
    places = own * held + jnp.arange(held, dtype=jnp.int32)
    match = (store_slot[None, :] == places[:, None]).astype(jnp.int32)
    held_id = jnp.sum(match * jnp.arange(store_slot.shape[0], dtype=jnp.int32)[None, :], axis=1)
    held_len = jnp.sum(match * lengths[None, :], axis=1)
    hit = jnp.any(passage_ids[:, :, None] == held_id[None, None, :], axis=1)
    turn = question[:, None] == jnp.arange(count, dtype=jnp.int32)[None, :]
    used = jnp.any(turn[:, :, None] & hit[None, :, :], axis=1).astype(jnp.int32)
    slot = jnp.sum(used * jnp.arange(held, dtype=jnp.int32)[None, :], axis=1)
    live_len = jnp.sum(used * held_len[None, :], axis=1)

    vmem = pl.BlockSpec(memory_space=pltpu.VMEM)
    smem = pl.BlockSpec(memory_space=pltpu.SMEM)
    dma = pltpu.SemaphoreType.DMA
    ranks = lax.axis_size("tensor")
    low, full = jnp.bfloat16, jnp.float32
    context, grad_queries, grad_keys, grad_values, mass = pl.pallas_call(
        functools.partial(kernel, ny, nx, ranks),
        in_specs=[smem, smem] + [vmem] * 4,
        out_specs=[vmem] * 5,
        out_shape=[jax.ShapeDtypeStruct(a.shape, a.dtype) for a in (queries, queries, keys, values)]
        + [jax.ShapeDtypeStruct((count, 128), full)],
        scratch_shapes=[
            pltpu.VMEM((count, target, feats), low),
            pltpu.VMEM((count, target, feats), low),
            pltpu.VMEM((held, heads * rows, feats), low),
            pltpu.VMEM((held, heads * rows, feats), low),
            pltpu.VMEM((held, feats, rows), low),
            pltpu.VMEM((held, feats, rows), low),
            pltpu.VMEM((count, 3 * heads, target), full),
            pltpu.VMEM((ny, nx, 3 * heads, target), full),
            pltpu.VMEM((ny, 3 * heads, target), full),
            pltpu.VMEM((ny, 3 * heads, target), full),
            pltpu.VMEM((nx, ny, 2 * heads, target), full),
            pltpu.VMEM((count, 2 * heads, target), full),
            pltpu.VMEM((count, target), full),
            pltpu.VMEM((count, 128), full),
            pltpu.VMEM((ranks, count, 128), full),
            pltpu.VMEM((count, feats, target), full),
            pltpu.VMEM((count, feats, target), full),
            pltpu.VMEM((entry_count, feats + 16, target), jnp.int16),
            pltpu.VMEM((entry_count, feats + 16, target), jnp.int16),
            pltpu.VMEM(keys.shape, full),
            pltpu.VMEM(values.shape, full),
            dma((len(slots), 4)),
            dma((len(slots), 4)),
            dma((ny, nx)),
            dma((ny, nx)),
        ]
        + [dma((ny,))] * 4
        + [dma((nx,))] * 2
        + [dma((ranks,))] * 2
        + [dma((entry_count,))] * 2,
        compiler_params=pltpu.CompilerParams(collective_id=0, has_side_effects=True, vmem_limit_bytes=61 << 20),
    )(slot, live_len, queries, cotangent, keys, values)
    relevance = jnp.sum(used.astype(full) * mass[:, :1], axis=0)
    return context, grad_queries, grad_keys, grad_values, relevance


def solution(mesh):
    wide = P("dp", None, "tensor")
    return jax.shard_map(
        local,
        mesh=mesh,
        in_specs=(wide, wide, wide, wide, P(), P(), P()),
        out_specs=(wide, wide, wide, wide, P("dp")),
        check_vma=False,
    )
```

```python
import functools

import jax
import jax.numpy as jnp
from jax import lax
from jax.experimental import pallas as pl
from jax.experimental.pallas import tpu as pltpu
from jax.sharding import PartitionSpec as P

HD = 64
SCALE = 0.125
NEG = -1e30
NX = 4
LAG = 2
STEPS = ((1, 0), (-1, 0), (0, 1), (0, -1))


def onward(kind, dy, dx, ny, nx):
    def along(near, size, plus_reach, plus_link):
        links = []
        minus_reach = size - 1 - plus_reach
        gone_plus, gone_minus = (-near) % size, near % size
        if gone_plus < plus_reach:
            links.append(plus_link)
        if gone_minus < minus_reach and (gone_plus == 0 or gone_plus > plus_reach):
            links.append(plus_link + 1)
        return links

    up = ny // 2
    if kind == 0:
        links = along(dx, nx, nx // 2 if dy % 4 != 3 else nx - 1 - nx // 2, 2)
        if dx == 0:
            links += along(dy, ny, up, 0)
        return links
    far = nx // 2
    plus = up if dx % 2 == 0 else ny - 1 - up
    gone_plus, gone_minus = (-dy) % ny, dy % ny
    near_row = gone_plus <= ny // 4 or gone_minus <= (ny - 1 - up) // 2
    links = along(dy, ny, plus, 0)
    if dx == far:
        links = [n for n in links if (gone_plus < ny // 4 if n == 0 else gone_minus < (ny - 1 - up) // 2)]
    if dy == 0:
        links += along(dx, nx, nx - 1 - far, 2)
    elif dx == far - 1 and not near_row:
        links.append(3)
    return links


@functools.lru_cache(maxsize=None)
def schedule(ny, nx):
    def moved(link, dy, dx):
        return ((dy - STEPS[link][0]) % ny, (dx - STEPS[link][1]) % nx)

    @functools.lru_cache(maxsize=None)
    def height(kind, dy, dx, link):
        to = moved(link, dy, dx)
        return 1 + max([height(kind, *to, n) for n in onward(kind, *to, ny, nx)], default=0)

    came = {(0, 0, 0): -LAG, (1, 0, 0): -LAG}
    todo = {(k, 0, 0, n) for k in (0, 1) for n in onward(k, 0, 0, ny, nx)}
    slots = []
    while todo:
        t = len(slots)
        now, fresh = [], {}
        for link in range(4):
            able = [j for j in todo if j[3] == link and came[j[:3]] <= t - LAG]
            if able:
                best = max(able, key=lambda j: (height(*j), j))
                todo.remove(best)
                to = moved(link, best[1], best[2])
                now.append((link, best[0], best[1:3], to))
                fresh[(best[0],) + to] = t
        came.update(fresh)
        for k, dy, dx in fresh:
            todo |= {(k, dy, dx, n) for n in onward(k, dy, dx, ny, nx)}
        slots.append(now)
    places = [(dy, dx) for dy in range(ny) for dx in range(nx)]
    ready = {p: max(came[(0,) + p], came[(1,) + p]) for p in places}
    order = sorted(places, key=lambda p: (ready[p], p))
    return slots, order, ready


def dot_nt(a, b):
    return lax.dot_general(a, b, (((1,), (1,)), ((), ())), preferred_element_type=jnp.float32)


def dot_nn(a, b):
    return lax.dot_general(a, b, (((1,), (0,)), ((), ())), preferred_element_type=jnp.float32)


def peer(ny, nx, dy, dx):
    own = lax.axis_index("dp")
    y, x = own // nx, own % nx
    return {"dp": ((y + dy) % ny) * nx + (x + dx) % nx}


def remote(src, dst, send_sem, recv_sem, device):
    return pltpu.make_async_remote_copy(
        src_ref=src, dst_ref=dst, send_sem=send_sem, recv_sem=recv_sem,
        device_id=device, device_id_type=pl.DeviceIdType.MESH,
    )


def pick_heads(stacked, lane):
    heads = len(stacked)
    out = stacked[heads - 1]
    for h in range(heads - 2, -1, -1):
        out = jnp.where(lane < (h + 1) * HD, stacked[h], out)
    return out


def merged(got, lines):
    top = jnp.max(got[..., :lines, :], axis=0)
    weight = jnp.exp(got[..., :lines, :] - top[None])
    total = jnp.sum(got[..., lines : 2 * lines, :] * weight, axis=0)
    delta = jnp.sum(got[..., 2 * lines :, :] * weight, axis=0)
    return top, total, delta


def kernel(
    ny, nx, ranks, slot_ref, len_ref, q_ref, g_ref, k_ref, v_ref,
    ctx_ref, gq_ref, dk_ref, dv_ref, mass_ref,
    aq, ag, km, vm, kt, vt, st, got_x, mid, got_y, fin_x, fin, mass_own, mass_got,
    own_o, own_q, sent_buf, got_buf, dk_acc, dv_acc,
    send_sem, recv_sem, sx_sem, rx_sem, sy_sem, ry_sem, sf_sem, rf_sem, sd_sem, rd_sem, sm_sem, rm_sem, sr_sem, rr_sem,
):
    slots, order, ready = schedule(ny, nx)
    index = {p: i for i, p in enumerate(order)}
    count = ny * nx
    length = len(slots)
    held, rows, _ = k_ref.shape
    target = q_ref.shape[1]
    width = aq.shape[2]
    heads = width // HD
    wraps = target // 128
    lines = heads * wraps
    rank = lax.axis_index("tensor")
    entries = [(t,) + e for t in range(length) for e in slots[t]]

    aq[0] = q_ref[0]
    ag[0] = g_ref[0]

    barrier = pltpu.get_barrier_semaphore()
    met = [peer(ny, nx, 0, dx) for dx in range(1, nx)] + [peer(ny, nx, dy, 0) for dy in range(1, ny)]
    met += [{"tensor": lax.rem(rank + r, ranks)} for r in range(1, ranks)]
    for device in met:
        pl.semaphore_signal(barrier, inc=1, device_id=device, device_id_type=pl.DeviceIdType.MESH)
    pl.semaphore_wait(barrier, len(met))

    def gathers(g):
        return [
            remote((aq, ag)[kind].at[index[sent]], (aq, ag)[kind].at[index[got]], send_sem.at[g, link],
                   recv_sem.at[g, link], peer(ny, nx, *STEPS[link]))
            for link, kind, sent, got in slots[g]
        ]

    def advance(g):
        if g >= LAG:
            for copy in gathers(g - LAG):
                copy.wait_recv()
        if g < length:
            for copy in gathers(g):
                copy.start()

    def stat_x(i):
        dy, dx = order[i]
        back = (-dx) % nx
        return remote(st.at[i], got_x.at[back, dy], sx_sem.at[dy, dx], rx_sem.at[dy, back], peer(ny, nx, 0, dx))

    def stat_y(dy):
        back = (-dy) % ny
        return remote(mid.at[dy], got_y.at[back], sy_sem.at[dy], ry_sem.at[back], peer(ny, nx, dy, 0))

    def fin_y(dy):
        back = (-dy) % ny
        return remote(fin_x.at[0, 0], fin_x.at[0, back], sf_sem.at[dy], rf_sem.at[back], peer(ny, nx, dy, 0))

    def fin_over_x(dy, dx):
        back = (-dx) % nx
        return remote(fin_x.at[0, dy], fin_x.at[back, dy], sd_sem.at[dy, dx], rd_sem.at[dy, back], peer(ny, nx, 0, dx))

    def stage(n):
        if n == 0:
            for i in range(count):
                if order[i][1]:
                    stat_x(i).wait_recv()
                else:
                    got_x[0, order[i][0]] = st[i]
            for k, stat in enumerate(merged(got_x[...], lines)):
                mid[:, k * lines : (k + 1) * lines] = stat
            for dy in range(1, ny):
                stat_y(dy).start()
            got_y[0] = mid[0]
        elif n == 1:
            for dy in range(1, ny):
                stat_y(dy).wait_recv()
            top, total, delta = merged(got_y[...], lines)
            fin_x[0, 0, :lines] = top + jnp.log(total)
            fin_x[0, 0, lines:] = delta / total
            for dy in range(1, ny):
                fin_y(dy).start()
            for dx in range(1, nx):
                fin_over_x(0, dx).start()
        elif n == 2:
            for dy in sorted(range(1, ny), key=lambda d: min(d, ny - d)):
                fin_y(-dy % ny).wait_recv()
                for dx in range(1, nx):
                    fin_over_x(dy, dx).start()
        else:
            for dx in range(1, nx):
                for dy in range(ny):
                    fin_over_x(dy, dx).wait_recv()
            for i, (dy, dx) in enumerate(order):
                fin[i] = fin_x[dx, dy]

    for g in range(LAG):
        advance(g)

    lane = lax.broadcasted_iota(jnp.int32, (rows, width), 1)
    for s in range(held):
        keys, values = k_ref[s].astype(jnp.float32), v_ref[s].astype(jnp.float32)
        kt[s] = keys.T.astype(jnp.bfloat16)
        vt[s] = values.T.astype(jnp.bfloat16)
        for h in range(heads):
            mine = (lane >= h * HD) & (lane < (h + 1) * HD)
            km[s, h * rows : (h + 1) * rows] = jnp.where(mine, keys * SCALE, 0.0).astype(jnp.bfloat16)
            vm[s, h * rows : (h + 1) * rows] = jnp.where(mine, values, 0.0).astype(jnp.bfloat16)

    live_row = lax.broadcasted_iota(jnp.int32, (rows, target), 0)

    def pass_one(i, carry):
        passed = LAG
        for c in range(1, count):
            upto = max(passed, ready[order[c]] + LAG + 1)
            if c == count - 1:
                upto = length + LAG

            @pl.when(i == c)
            def _():
                for g in range(passed, upto):
                    advance(g)
                if order[c - 1][1]:
                    stat_x(c - 1).start()

            passed = upto
        slot = slot_ref[i]
        live = live_row < len_ref[i]
        all_scores = dot_nt(km[slot], aq[i])
        all_grads = dot_nt(vm[slot], ag[i])
        for h in range(heads):
            cut = slice(h * rows, (h + 1) * rows)
            scores = jnp.where(live, all_scores[cut], NEG)
            top = jnp.max(scores, axis=0, keepdims=True)
            raised = jnp.exp(scores - top)
            total = jnp.sum(raised, axis=0, keepdims=True)
            delta = jnp.sum(raised * all_grads[cut], axis=0, keepdims=True)
            for k, stat in enumerate((top, total, delta)):
                for w in range(wraps):
                    line = k * lines + h * wraps + w
                    st[i, line : line + 1] = stat[:, w * 128 : (w + 1) * 128]
        return carry

    lax.fori_loop(0, count, pass_one, 0)
    if order[count - 1][1]:
        stat_x(count - 1).start()
    for n in range(4):
        stage(n)

    share = jnp.sum(st[:, lines : 2 * lines] * jnp.exp(st[:, :lines] - fin[:, :lines]), axis=1)
    per_row = jnp.sum(share, axis=1, keepdims=True)
    diagonal = lax.broadcasted_iota(jnp.int32, (count, 128), 0) == lax.broadcasted_iota(jnp.int32, (count, 128), 1)
    mass_own[...] = jnp.broadcast_to(jnp.sum(jnp.where(diagonal, per_row, 0.0), axis=0, keepdims=True), mass_own.shape)

    def masses(r):
        return remote(mass_own, mass_got.at[r], sm_sem.at[r], rm_sem.at[r], {"tensor": lax.rem(rank + r, ranks)})

    for r in range(1, ranks):
        masses(r).start()

    owns = (own_o, own_q)

    def copy_of(n):
        link = entries[n][1]
        return remote(sent_buf.at[n], got_buf.at[n], sr_sem.at[n], rr_sem.at[n], peer(ny, nx, -STEPS[link][0], -STEPS[link][1]))

    def summed(kind, place):
        kids = [n for n, (_, _, k, sent, _) in enumerate(entries) if k == kind and sent == place]
        for n in kids:
            copy_of(n).wait_recv()
        powers = [jnp.exp2(got_buf[n, width : width + 16, :].astype(jnp.float32)) for n in kids]
        for h in range(heads):
            cut = slice(h * HD, (h + 1) * HD)
            acc = owns[kind][index[place], cut, :]
            for n, power in zip(kids, powers):
                acc = acc + got_buf[n, cut, :].astype(jnp.float32) * power[h : h + 1]
            yield cut, acc

    row16 = lax.broadcasted_iota(jnp.int32, (16, target), 0)

    def send_on(n):
        _, _, kind, _, place = entries[n]
        shifts = jnp.zeros((16, target), jnp.float32)
        for h, (cut, acc) in enumerate(summed(kind, place)):
            most = jnp.maximum(jnp.max(jnp.abs(acc), axis=0, keepdims=True), 1e-30)
            shift = jnp.ceil(jnp.log2(most) + 0.01) - 15.0
            coded = jnp.floor(acc * jnp.exp2(-shift) + 0.5)
            sent_buf[n, cut, :] = coded.astype(jnp.int32).astype(jnp.int16)
            shifts = jnp.where(row16 == h, shift, shifts)
        sent_buf[n, width : width + 16, :] = shifts.astype(jnp.int32).astype(jnp.int16)
        copy_of(n).start()

    dk_acc[...] = jnp.zeros_like(dk_acc)
    dv_acc[...] = jnp.zeros_like(dv_acc)

    def pass_two(step, carry):
        i = count - 1 - step
        slot = slot_ref[i]
        live = live_row < len_ref[i]
        queries = aq[i]
        grads = ag[i]
        all_scores = dot_nt(km[slot], queries)
        all_grads = dot_nt(vm[slot], grads)
        dks, dvs = [], []
        for h in range(heads):
            cut = slice(h * HD, (h + 1) * HD)
            log_sum, delta = [
                jnp.concatenate([fin[i, k * lines + h * wraps + w][None] for w in range(wraps)], axis=1)
                for k in range(2)
            ]
            prob = jnp.where(live, jnp.exp(all_scores[h * rows : (h + 1) * rows] - log_sum), 0.0)
            low = prob.astype(jnp.bfloat16)
            gs = (prob * (all_grads[h * rows : (h + 1) * rows] - delta)).astype(jnp.bfloat16)
            own_o[i, cut, :] = dot_nn(vt[slot, cut, :], low)
            own_q[i, cut, :] = dot_nn(kt[slot, cut, :], gs)
            dks.append(dot_nn(gs, queries))
            dvs.append(dot_nn(low, grads))
        dk = (pick_heads(dks, lane) * SCALE).astype(jnp.bfloat16).astype(jnp.float32)
        dv = pick_heads(dvs, lane).astype(jnp.bfloat16).astype(jnp.float32)
        for s in range(held):
            mine = jnp.where(slot == s, 1.0, 0.0)
            dk_acc[s] += dk * mine
            dv_acc[s] += dv * mine

        passed = 0
        for c in range(count):
            upto = passed
            while upto < length and all(index[e[3]] >= count - 1 - c for e in slots[length - 1 - upto]):
                upto += 1
            if upto > passed:

                @pl.when(step == c)
                def _():
                    for u in range(passed, upto):
                        for n, e in enumerate(entries):
                            if e[0] == length - 1 - u:
                                send_on(n)

                passed = upto
        return carry

    lax.fori_loop(0, count, pass_two, 0)

    dk_ref[...] = dk_acc[...].astype(jnp.bfloat16)
    dv_ref[...] = dv_acc[...].astype(jnp.bfloat16)
    for kind, out, factor in ((0, ctx_ref, 1.0), (1, gq_ref, SCALE)):
        whole = jnp.concatenate([acc for _, acc in summed(kind, (0, 0))], axis=0)
        out[0] = (whole.T * factor).astype(jnp.bfloat16)
    mass = mass_own[...]
    for r in range(1, ranks):
        masses(r).wait_recv()
        mass = mass + mass_got[r]
    mass_ref[...] = (mass / (target * heads * ranks)).astype(jnp.bfloat16).astype(jnp.float32)

    for g in range(length):
        for copy in gathers(g):
            copy.wait_send()
    for r in range(1, ranks):
        masses(r).wait_send()
    for i in range(count):
        if order[i][1]:
            stat_x(i).wait_send()
    for dy in range(ny):
        if dy:
            stat_y(dy).wait_send()
            fin_y(dy).wait_send()
        for dx in range(1, nx):
            fin_over_x(dy, dx).wait_send()
    for n in range(len(entries)):
        copy_of(n).wait_send()


def hand_over(*refs):
    for n in range(len(refs) // 2):
        refs[len(refs) // 2 + n][...] = refs[n][...]


def local(queries, keys, values, cotangent, passage_ids, store_slot, lengths):
    own = lax.axis_index("dp")
    count = lax.axis_size("dp")
    nx = NX
    ny = count // nx
    slots, order, _ = schedule(ny, nx)
    entry_count = sum(len(s) for s in slots)
    held, rows, feats = keys.shape
    target = queries.shape[1]
    heads = feats // HD

    dys = jnp.array([p[0] for p in order], jnp.int32)
    dxs = jnp.array([p[1] for p in order], jnp.int32)
    question = ((own // nx + dys) % ny) * nx + (own % nx + dxs) % nx
    places = own * held + jnp.arange(held, dtype=jnp.int32)
    match = (store_slot[None, :] == places[:, None]).astype(jnp.int32)
    held_id = jnp.sum(match * jnp.arange(store_slot.shape[0], dtype=jnp.int32)[None, :], axis=1)
    held_len = jnp.sum(match * lengths[None, :], axis=1)
    hit = jnp.any(passage_ids[:, :, None] == held_id[None, None, :], axis=1)
    turn = question[:, None] == jnp.arange(count, dtype=jnp.int32)[None, :]
    used = jnp.any(turn[:, :, None] & hit[None, :, :], axis=1).astype(jnp.int32)
    slot = jnp.sum(used * jnp.arange(held, dtype=jnp.int32)[None, :], axis=1)
    live_len = jnp.sum(used * held_len[None, :], axis=1)

    vmem = pl.BlockSpec(memory_space=pltpu.VMEM)
    smem = pl.BlockSpec(memory_space=pltpu.SMEM)
    dma = pltpu.SemaphoreType.DMA
    ranks = lax.axis_size("tensor")
    low, full = jnp.bfloat16, jnp.float32
    heads = feats // HD
    lines = heads * target // 128
    outs = [jax.ShapeDtypeStruct(a.shape, a.dtype) for a in (queries, queries, keys, values)]
    *results, mass = pl.pallas_call(
        functools.partial(kernel, ny, nx, ranks),
        in_specs=[smem, smem] + [vmem] * 4,
        out_specs=[vmem] * 5,
        out_shape=outs + [jax.ShapeDtypeStruct((8, 128), full)],
        scratch_shapes=[
            pltpu.VMEM((count, target, feats), low),
            pltpu.VMEM((count, target, feats), low),
            pltpu.VMEM((held, heads * rows, feats), low),
            pltpu.VMEM((held, heads * rows, feats), low),
            pltpu.VMEM((held, feats, rows), low),
            pltpu.VMEM((held, feats, rows), low),
            pltpu.VMEM((count, 3 * lines, 128), full),
            pltpu.VMEM((nx, ny, 3 * lines, 128), full),
            pltpu.VMEM((ny, 3 * lines, 128), full),
            pltpu.VMEM((ny, 3 * lines, 128), full),
            pltpu.VMEM((nx, ny, 2 * lines, 128), full),
            pltpu.VMEM((count, 2 * lines, 128), full),
            pltpu.VMEM((8, 128), full),
            pltpu.VMEM((ranks, 8, 128), full),
            pltpu.VMEM((count, feats, target), full),
            pltpu.VMEM((count, feats, target), full),
            pltpu.VMEM((entry_count, feats + 16, target), jnp.int16),
            pltpu.VMEM((entry_count, feats + 16, target), jnp.int16),
            pltpu.VMEM((held, rows, feats), full),
            pltpu.VMEM((held, rows, feats), full),
            dma((len(slots), 4)),
            dma((len(slots), 4)),
            dma((ny, nx)),
            dma((ny, nx)),
        ]
        + [dma((ny,))] * 4
        + [dma((ny, nx))] * 2
        + [dma((ranks,))] * 2
        + [dma((entry_count,))] * 2,
        compiler_params=pltpu.CompilerParams(collective_id=0, has_side_effects=True, vmem_limit_bytes=62 << 20),
    )(slot, live_len, queries, cotangent, keys, values)
    context, grad_queries, grad_keys, grad_values = pl.pallas_call(
        hand_over,
        in_specs=[vmem] * 4,
        out_specs=[vmem] * 4,
        out_shape=outs,
        compiler_params=pltpu.CompilerParams(vmem_limit_bytes=16 << 20),
    )(*results)
    relevance = jnp.sum(used.astype(full) * mass[0, :count, None], axis=0)
    return context, grad_queries, grad_keys, grad_values, relevance


def solution(mesh):
    wide = P("dp", None, "tensor")
    return jax.shard_map(
        local,
        mesh=mesh,
        in_specs=(wide, wide, wide, wide, P(), P(), P()),
        out_specs=(wide, wide, wide, wide, P("dp")),
        check_vma=False,
    )
```

```python
import functools

import jax
import jax.numpy as jnp
from jax import lax
from jax.experimental import pallas as pl
from jax.experimental.pallas import tpu as pltpu
from jax.sharding import PartitionSpec as P

HD = 64
SCALE = 0.125
NEG = -1e30
NX = 4
LAG = 3
STEPS = ((1, 0), (-1, 0), (0, 1), (0, -1))


def onward(kind, dy, dx, ny, nx):
    def along(near, size, plus_reach, plus_link):
        links = []
        minus_reach = size - 1 - plus_reach
        gone_plus, gone_minus = (-near) % size, near % size
        if gone_plus < plus_reach:
            links.append(plus_link)
        if gone_minus < minus_reach and (gone_plus == 0 or gone_plus > plus_reach):
            links.append(plus_link + 1)
        return links

    up = ny // 2
    if kind == 0:
        links = along(dx, nx, nx // 2 if dy % 4 != 3 else nx - 1 - nx // 2, 2)
        if dx == 0:
            links += along(dy, ny, up, 0)
        return links
    far = nx // 2
    plus = up if dx % 2 == 0 else ny - 1 - up
    gone_plus, gone_minus = (-dy) % ny, dy % ny
    near_row = gone_plus <= ny // 4 or gone_minus <= (ny - 1 - up) // 2
    links = along(dy, ny, plus, 0)
    if dx == far:
        links = [n for n in links if (gone_plus < ny // 4 if n == 0 else gone_minus < (ny - 1 - up) // 2)]
    if dy == 0:
        links += along(dx, nx, nx - 1 - far, 2)
    elif dx == far - 1 and not near_row:
        links.append(3)
    return links


@functools.lru_cache(maxsize=None)
def schedule(ny, nx):
    def moved(link, dy, dx):
        return ((dy - STEPS[link][0]) % ny, (dx - STEPS[link][1]) % nx)

    @functools.lru_cache(maxsize=None)
    def height(kind, dy, dx, link):
        to = moved(link, dy, dx)
        return 1 + max([height(kind, *to, n) for n in onward(kind, *to, ny, nx)], default=0)

    came = {(0, 0, 0): -LAG, (1, 0, 0): -LAG}
    todo = {(k, 0, 0, n) for k in (0, 1) for n in onward(k, 0, 0, ny, nx)}
    slots = []
    while todo:
        t = len(slots)
        now, fresh = [], {}
        for link in range(4):
            able = [j for j in todo if j[3] == link and came[j[:3]] <= t - LAG]
            if able:
                best = max(able, key=lambda j: (height(*j), j))
                todo.remove(best)
                to = moved(link, best[1], best[2])
                now.append((link, best[0], best[1:3], to))
                fresh[(best[0],) + to] = t
        came.update(fresh)
        for k, dy, dx in fresh:
            todo |= {(k, dy, dx, n) for n in onward(k, dy, dx, ny, nx)}
        slots.append(now)
    places = [(dy, dx) for dy in range(ny) for dx in range(nx)]
    ready = {p: max(came[(0,) + p], came[(1,) + p]) for p in places}
    order = sorted(places, key=lambda p: (ready[p], p))
    return slots, order, ready


def dot_nt(a, b):
    return lax.dot_general(a, b, (((1,), (1,)), ((), ())), preferred_element_type=jnp.float32)


def dot_nn(a, b):
    return lax.dot_general(a, b, (((1,), (0,)), ((), ())), preferred_element_type=jnp.float32)


def peer(ny, nx, dy, dx):
    own = lax.axis_index("dp")
    y, x = own // nx, own % nx
    return {"dp": ((y + dy) % ny) * nx + (x + dx) % nx}


def remote(src, dst, send_sem, recv_sem, device):
    return pltpu.make_async_remote_copy(
        src_ref=src, dst_ref=dst, send_sem=send_sem, recv_sem=recv_sem,
        device_id=device, device_id_type=pl.DeviceIdType.MESH,
    )


def pick_heads(stacked, lane):
    heads = len(stacked)
    out = stacked[heads - 1]
    for h in range(heads - 2, -1, -1):
        out = jnp.where(lane < (h + 1) * HD, stacked[h], out)
    return out


def merged(got, lines):
    top = jnp.max(got[..., :lines, :], axis=0)
    weight = jnp.exp(got[..., :lines, :] - top[None])
    total = jnp.sum(got[..., lines : 2 * lines, :] * weight, axis=0)
    delta = jnp.sum(got[..., 2 * lines :, :] * weight, axis=0)
    return top, total, delta


def kernel(
    ny, nx, ranks, ids_ref, store_ref, length_ref, q_ref, g_ref, k_ref, v_ref,
    ctx_ref, gq_ref, dk_ref, dv_ref, rel_ref,
    slot_ref, len_ref,
    aq, ag, km, vm, kt, vt, st, got_x, mid, got_y, fin_x, fin, mass_own, mass_got,
    own_o, own_q, sent_buf, got_buf, dk_acc, dv_acc,
    send_sem, recv_sem, sx_sem, rx_sem, sy_sem, ry_sem, sf_sem, rf_sem, sd_sem, rd_sem, sm_sem, rm_sem, sr_sem, rr_sem,
):
    slots, order, ready = schedule(ny, nx)
    index = {p: i for i, p in enumerate(order)}
    count = ny * nx
    length = len(slots)
    held, rows, _ = k_ref.shape
    target = q_ref.shape[1]
    width = aq.shape[2]
    heads = width // HD
    wraps = target // 128
    lines = heads * wraps
    rank = lax.axis_index("tensor")
    entries = [(t,) + e for t in range(length) for e in slots[t]]

    aq[0] = q_ref[0]
    ag[0] = g_ref[0]

    barrier = pltpu.get_barrier_semaphore()
    met = [peer(ny, nx, 0, dx) for dx in range(1, nx)] + [peer(ny, nx, dy, 0) for dy in range(1, ny)]
    met += [{"tensor": lax.rem(rank + r, ranks)} for r in range(1, ranks)]
    for device in met:
        pl.semaphore_signal(barrier, inc=1, device_id=device, device_id_type=pl.DeviceIdType.MESH)
    pl.semaphore_wait(barrier, len(met))

    def gathers(g):
        return [
            remote((aq, ag)[kind].at[index[sent]], (aq, ag)[kind].at[index[got]], send_sem.at[g, link],
                   recv_sem.at[g, link], peer(ny, nx, *STEPS[link]))
            for link, kind, sent, got in slots[g]
        ]

    def advance(g):
        if g >= LAG:
            for copy in gathers(g - LAG):
                copy.wait_recv()
        if g < length:
            for copy in gathers(g):
                copy.start()

    def stat_x(i):
        dy, dx = order[i]
        back = (-dx) % nx
        return remote(st.at[i], got_x.at[back, dy], sx_sem.at[dy, dx], rx_sem.at[dy, back], peer(ny, nx, 0, dx))

    def stat_y(dy):
        back = (-dy) % ny
        return remote(mid.at[dy], got_y.at[back], sy_sem.at[dy], ry_sem.at[back], peer(ny, nx, dy, 0))

    def fin_y(dy):
        back = (-dy) % ny
        return remote(fin_x.at[0, 0], fin_x.at[0, back], sf_sem.at[dy], rf_sem.at[back], peer(ny, nx, dy, 0))

    def fin_over_x(dy, dx):
        back = (-dx) % nx
        return remote(fin_x.at[0, dy], fin_x.at[back, dy], sd_sem.at[dy, dx], rd_sem.at[dy, back], peer(ny, nx, 0, dx))

    def stage(n):
        if n == 0:
            for i in range(count):
                if order[i][1]:
                    stat_x(i).wait_recv()
                else:
                    got_x[0, order[i][0]] = st[i]
            for k, stat in enumerate(merged(got_x[...], lines)):
                mid[:, k * lines : (k + 1) * lines] = stat
            for dy in range(1, ny):
                stat_y(dy).start()
            got_y[0] = mid[0]
        elif n == 1:
            for dy in range(1, ny):
                stat_y(dy).wait_recv()
            top, total, delta = merged(got_y[...], lines)
            fin_x[0, 0, :lines] = top + jnp.log(total)
            fin_x[0, 0, lines:] = delta / total
            for dy in range(1, ny):
                fin_y(dy).start()
            for dx in range(1, nx):
                fin_over_x(0, dx).start()
        elif n == 2:
            for dy in sorted(range(1, ny), key=lambda d: min(d, ny - d)):
                fin_y(-dy % ny).wait_recv()
                for dx in range(1, nx):
                    fin_over_x(dy, dx).start()
        else:
            for dx in range(1, nx):
                for dy in range(ny):
                    fin_over_x(dy, dx).wait_recv()
            for i, (dy, dx) in enumerate(order):
                fin[i] = fin_x[dx, dy]

    for g in range(LAG):
        advance(g)

    lane = lax.broadcasted_iota(jnp.int32, (rows, width), 1)
    for s in range(held):
        keys, values = k_ref[s].astype(jnp.float32), v_ref[s].astype(jnp.float32)
        kt[s] = keys.T.astype(jnp.bfloat16)
        vt[s] = values.T.astype(jnp.bfloat16)
        for h in range(heads):
            mine = (lane >= h * HD) & (lane < (h + 1) * HD)
            km[s, h * rows : (h + 1) * rows] = jnp.where(mine, keys * SCALE, 0.0).astype(jnp.bfloat16)
            vm[s, h * rows : (h + 1) * rows] = jnp.where(mine, values, 0.0).astype(jnp.bfloat16)

    live_row = lax.broadcasted_iota(jnp.int32, (rows, target), 0)

    own = lax.axis_index("dp")
    lane_one = lax.broadcasted_iota(jnp.int32, (1, 128), 1)

    def pass_one(i, carry):
        passed = LAG
        for c in range(1, count):
            upto = max(passed, ready[order[c]] + LAG + 1)
            if c == count - 1:
                upto = length + LAG

            @pl.when(i == c)
            def _():
                for g in range(passed, upto):
                    advance(g)
                if order[c - 1][1]:
                    stat_x(c - 1).start()

            passed = upto
        dy = dx = 0
        for c in range(1, count):
            dy = jnp.where(i == c, order[c][0], dy)
            dx = jnp.where(i == c, order[c][1], dx)
        question = ((own // nx + dy) % ny) * nx + (own % nx + dx) % nx
        slot = live_len = 0
        for n in range(ids_ref.shape[1]):
            passage = ids_ref[question, n]
            near = store_ref[passage] - own * held
            mine = (near >= 0) & (near < held)
            slot += jnp.where(mine, near, 0)
            live_len += jnp.where(mine, length_ref[passage], 0)
        slot_ref[i] = slot
        len_ref[i] = live_len
        live = live_row < live_len
        all_scores = dot_nt(km[slot], aq[i])
        all_grads = dot_nt(vm[slot], ag[i])
        for h in range(heads):
            cut = slice(h * rows, (h + 1) * rows)
            scores = jnp.where(live, all_scores[cut], NEG)
            top = jnp.max(scores, axis=0, keepdims=True)
            raised = jnp.exp(scores - top)
            total = jnp.sum(raised, axis=0, keepdims=True)
            delta = jnp.sum(raised * all_grads[cut], axis=0, keepdims=True)
            for k, stat in enumerate((top, total, delta)):
                for w in range(wraps):
                    line = k * lines + h * wraps + w
                    st[i, line : line + 1] = stat[:, w * 128 : (w + 1) * 128]
        return carry

    lax.fori_loop(0, count, pass_one, 0)
    if order[count - 1][1]:
        stat_x(count - 1).start()
    for n in range(4):
        stage(n)

    share = jnp.sum(st[:, lines : 2 * lines] * jnp.exp(st[:, :lines] - fin[:, :lines]), axis=1)
    per_row = jnp.sum(share, axis=1, keepdims=True)
    diagonal = lax.broadcasted_iota(jnp.int32, (count, 128), 0) == lax.broadcasted_iota(jnp.int32, (count, 128), 1)
    mass_own[...] = jnp.broadcast_to(jnp.sum(jnp.where(diagonal, per_row, 0.0), axis=0, keepdims=True), mass_own.shape)

    def masses(r):
        return remote(mass_own, mass_got.at[r], sm_sem.at[r], rm_sem.at[r], {"tensor": lax.rem(rank + r, ranks)})

    for r in range(1, ranks):
        masses(r).start()

    owns = (own_o, own_q)

    def copy_of(n):
        link = entries[n][1]
        return remote(sent_buf.at[n], got_buf.at[n], sr_sem.at[n], rr_sem.at[n], peer(ny, nx, -STEPS[link][0], -STEPS[link][1]))

    def summed(kind, place):
        kids = [n for n, (_, _, k, sent, _) in enumerate(entries) if k == kind and sent == place]
        for n in kids:
            copy_of(n).wait_recv()
        powers = [jnp.exp2(got_buf[n, width : width + 16, :].astype(jnp.float32)) for n in kids]
        for h in range(heads):
            cut = slice(h * HD, (h + 1) * HD)
            acc = owns[kind][index[place], cut, :]
            for n, power in zip(kids, powers):
                acc = acc + got_buf[n, cut, :].astype(jnp.float32) * power[h : h + 1]
            yield cut, acc

    row16 = lax.broadcasted_iota(jnp.int32, (16, target), 0)

    def send_on(n):
        _, _, kind, _, place = entries[n]
        shifts = jnp.zeros((16, target), jnp.float32)
        for h, (cut, acc) in enumerate(summed(kind, place)):
            most = jnp.maximum(jnp.max(jnp.abs(acc), axis=0, keepdims=True), 1e-30)
            shift = jnp.ceil(jnp.log2(most) + 0.01) - 15.0
            coded = jnp.floor(acc * jnp.exp2(-shift) + 0.5)
            sent_buf[n, cut, :] = coded.astype(jnp.int32).astype(jnp.int16)
            shifts = jnp.where(row16 == h, shift, shifts)
        sent_buf[n, width : width + 16, :] = shifts.astype(jnp.int32).astype(jnp.int16)
        copy_of(n).start()

    dk_acc[...] = jnp.zeros_like(dk_acc)
    dv_acc[...] = jnp.zeros_like(dv_acc)

    def pass_two(step, carry):
        i = count - 1 - step
        slot = slot_ref[i]
        live = live_row < len_ref[i]
        queries = aq[i]
        grads = ag[i]
        all_scores = dot_nt(km[slot], queries)
        all_grads = dot_nt(vm[slot], grads)
        dks, dvs = [], []
        for h in range(heads):
            cut = slice(h * HD, (h + 1) * HD)
            log_sum, delta = [
                jnp.concatenate([fin[i, k * lines + h * wraps + w][None] for w in range(wraps)], axis=1)
                for k in range(2)
            ]
            prob = jnp.where(live, jnp.exp(all_scores[h * rows : (h + 1) * rows] - log_sum), 0.0)
            low = prob.astype(jnp.bfloat16)
            gs = (prob * (all_grads[h * rows : (h + 1) * rows] - delta)).astype(jnp.bfloat16)
            own_o[i, cut, :] = dot_nn(vt[slot, cut, :], low)
            own_q[i, cut, :] = dot_nn(kt[slot, cut, :], gs)
            dks.append(dot_nn(gs, queries))
            dvs.append(dot_nn(low, grads))
        dk = (pick_heads(dks, lane) * SCALE).astype(jnp.bfloat16).astype(jnp.float32)
        dv = pick_heads(dvs, lane).astype(jnp.bfloat16).astype(jnp.float32)
        for s in range(held):
            mine = jnp.where(slot == s, 1.0, 0.0)
            dk_acc[s] += dk * mine
            dv_acc[s] += dv * mine

        passed = 0
        for c in range(count):
            upto = passed
            while upto < length and all(index[e[3]] >= count - 1 - c for e in slots[length - 1 - upto]):
                upto += 1
            if upto > passed:

                @pl.when(step == c)
                def _():
                    for u in range(passed, upto):
                        for n, e in enumerate(entries):
                            if e[0] == length - 1 - u:
                                send_on(n)

                passed = upto
        return carry

    lax.fori_loop(0, count, pass_two, 0)

    dk_ref[...] = dk_acc[...].astype(jnp.bfloat16)
    dv_ref[...] = dv_acc[...].astype(jnp.bfloat16)
    for kind, out, factor in ((0, ctx_ref, 1.0), (1, gq_ref, SCALE)):
        whole = jnp.concatenate([acc for _, acc in summed(kind, (0, 0))], axis=0)
        out[0] = (whole.T * factor).astype(jnp.bfloat16)
    mass = mass_own[...]
    for r in range(1, ranks):
        masses(r).wait_recv()
        mass = mass + mass_got[r]
    mass = (mass / (target * heads * ranks)).astype(jnp.bfloat16).astype(jnp.float32)[:1]
    place = jnp.full((1, 128), held, jnp.int32)
    for i in range(count):
        place = jnp.where(lane_one == i, jnp.where(len_ref[i] > 0, slot_ref[i], held), place)
    relevance = jnp.zeros((1, 128), jnp.float32)
    for s in range(held):
        received = jnp.sum(jnp.where(place == s, mass, 0.0), axis=1, keepdims=True)
        relevance = jnp.where(lane_one == s, received, relevance)
    rel_ref[...] = jnp.broadcast_to(relevance, rel_ref.shape)

    for g in range(length):
        for copy in gathers(g):
            copy.wait_send()
    for r in range(1, ranks):
        masses(r).wait_send()
    for i in range(count):
        if order[i][1]:
            stat_x(i).wait_send()
    for dy in range(ny):
        if dy:
            stat_y(dy).wait_send()
            fin_y(dy).wait_send()
        for dx in range(1, nx):
            fin_over_x(dy, dx).wait_send()
    for n in range(len(entries)):
        copy_of(n).wait_send()


def hand_over(*refs):
    for n in range(len(refs) // 2):
        refs[len(refs) // 2 + n][...] = refs[n][...]


def local(queries, keys, values, cotangent, passage_ids, store_slot, lengths):
    count = lax.axis_size("dp")
    nx = NX
    ny = count // nx
    slots, order, _ = schedule(ny, nx)
    entry_count = sum(len(s) for s in slots)
    held, rows, feats = keys.shape
    target = queries.shape[1]
    heads = feats // HD

    vmem = pl.BlockSpec(memory_space=pltpu.VMEM)
    smem = pl.BlockSpec(memory_space=pltpu.SMEM)
    dma = pltpu.SemaphoreType.DMA
    ranks = lax.axis_size("tensor")
    low, full = jnp.bfloat16, jnp.float32
    heads = feats // HD
    lines = heads * target // 128
    outs = [jax.ShapeDtypeStruct(a.shape, a.dtype) for a in (queries, queries, keys, values)]
    *results, received = pl.pallas_call(
        functools.partial(kernel, ny, nx, ranks),
        in_specs=[smem] * 3 + [vmem] * 4,
        out_specs=[vmem] * 5,
        out_shape=outs + [jax.ShapeDtypeStruct((8, 128), full)],
        scratch_shapes=[
            pltpu.SMEM((count,), jnp.int32),
            pltpu.SMEM((count,), jnp.int32),
            pltpu.VMEM((count, target, feats), low),
            pltpu.VMEM((count, target, feats), low),
            pltpu.VMEM((held, heads * rows, feats), low),
            pltpu.VMEM((held, heads * rows, feats), low),
            pltpu.VMEM((held, feats, rows), low),
            pltpu.VMEM((held, feats, rows), low),
            pltpu.VMEM((count, 3 * lines, 128), full),
            pltpu.VMEM((nx, ny, 3 * lines, 128), full),
            pltpu.VMEM((ny, 3 * lines, 128), full),
            pltpu.VMEM((ny, 3 * lines, 128), full),
            pltpu.VMEM((nx, ny, 2 * lines, 128), full),
            pltpu.VMEM((count, 2 * lines, 128), full),
            pltpu.VMEM((8, 128), full),
            pltpu.VMEM((ranks, 8, 128), full),
            pltpu.VMEM((count, feats, target), full),
            pltpu.VMEM((count, feats, target), full),
            pltpu.VMEM((entry_count, feats + 16, target), jnp.int16),
            pltpu.VMEM((entry_count, feats + 16, target), jnp.int16),
            pltpu.VMEM((held, rows, feats), full),
            pltpu.VMEM((held, rows, feats), full),
            dma((len(slots), 4)),
            dma((len(slots), 4)),
            dma((ny, nx)),
            dma((ny, nx)),
        ]
        + [dma((ny,))] * 4
        + [dma((ny, nx))] * 2
        + [dma((ranks,))] * 2
        + [dma((entry_count,))] * 2,
        compiler_params=pltpu.CompilerParams(collective_id=0, has_side_effects=True, vmem_limit_bytes=62 << 20),
    )(passage_ids, store_slot, lengths, queries, cotangent, keys, values)
    context, grad_queries, grad_keys, grad_values = pl.pallas_call(
        hand_over,
        in_specs=[vmem] * 4,
        out_specs=[vmem] * 4,
        out_shape=outs,
        compiler_params=pltpu.CompilerParams(vmem_limit_bytes=60 << 20),
    )(*results)
    return context, grad_queries, grad_keys, grad_values, received[0, :held]


def solution(mesh):
    wide = P("dp", None, "tensor")
    return jax.shard_map(
        local,
        mesh=mesh,
        in_specs=(wide, wide, wide, wide, P(), P(), P()),
        out_specs=(wide, wide, wide, wide, P("dp")),
        check_vma=False,
    )
```
